32 devices in a mesh: row: 4 (over z), col: 8 (over y, x, core).
Axes of the slice: x: 2, y: 2, z: 4, core: 2. Of those that a mesh axis runs over, the one named last changes fastest.
Arguments:
- activations: bfloat16 [1024, 5120], P('row', 'col'), may hold values from -6 to 6
- up_weight: bfloat16 [5120, 6912], P('row', 'col'), may hold values from -0.078125 to 0.078125
- hidden_cot: bfloat16 [1024, 6912], P('row', 'col'), may hold values from -6 to 6
Outputs:
- hidden: bfloat16 [1024, 6912], P('row', 'col')
- input_grad: bfloat16 [1024, 5120], P(('row', 'col'))
- weight_grad: float32 [5120, 6912], P('row', 'col')
The draws below stay inside these ranges and needn't reach their ends.
All inputs are finite; a program needn't handle non-finite values.
Results may differ from the reference program's by a relative error of at most 0.022.
Values may be sent and summed in bfloat16 or wider, within the bound.
No kernel may reach another device: no remote copies, remote signals or barrier semaphores. Data moves between devices by JAX's collectives and lax.ppermute only.
A program may use at most 64 MiB of HBM per device.

```python
import jax
import jax.numpy as jnp
from jax import lax

D = 5120
FF = 6912
TOK = 256
TOKENS = 1024
N_ROW = 4
N_COL = 8


def spiked(drawn, key, source, target, shards_of, factor):
    def block_of(axis_at):
        return (jnp.arange(drawn.shape[axis_at]) // (drawn.shape[axis_at] // shards_of)).reshape((-1,) + (1,) * (drawn.ndim - 1 - axis_at))

    near = jax.random.permutation(key, shards_of)[block_of(target)]
    second = (block_of(target) + shards_of // 2) % shards_of
    return jnp.where((block_of(source) == near) | (block_of(source) == second), factor * drawn, drawn)


def shard_levels(key, dims, split, smallest, top_value):
    factor_of = 1.0
    for dim, shards_of in split:
        steps = jax.random.uniform(jax.random.fold_in(jax.random.fold_in(key, 6), dim), (shards_of,), jnp.float32, smallest / len(split), top_value / len(split))
        factor_of = factor_of * jnp.repeat(jnp.exp(steps), dims[dim] // shards_of).reshape((-1,) + (1,) * (len(dims) - 1 - dim))
    return factor_of


def centred(own_key, dims, scale, reach, cuts=(), held_as=jnp.bfloat16):
    values = scale * jax.random.normal(own_key, dims, jnp.float32)
    if cuts:
        values = values * shard_levels(own_key, dims, cuts, -0.22, 0.18)
    return jnp.clip(values, -reach, reach).astype(held_as)


def noise_with(key, extent, deviation, most, shards, heavy, kind=jnp.bfloat16):
    entries = deviation * jax.random.normal(key, extent, jnp.float32)
    if shards:
        entries = entries * shard_levels(key, extent, shards, -0.22, 0.18)
    return jnp.clip(spiked(entries, jax.random.fold_in(key, 3), *heavy), -most, most).astype(kind)


def setup_inputs(seed: int = 0) -> dict:
    keys = jax.random.split(jax.random.key(seed), 4)
    return {
        "activations": noise_with(keys[0], (TOKENS, D), 1.0, 6.0, ((0, 4), (1, 8)), (0, 1, 8, 2.0)),
        "up_weight": centred(keys[1], (D, FF), D ** -0.5, 0.078125, ((0, 4), (1, 8))),
        "hidden_cot": noise_with(keys[2], (TOKENS, FF), 1.0, 6.0, ((0, 4), (1, 8)), (1, 0, 8, 2.0)),
    }


grad_scale = 0.015625

def gelu_tanh(value):
    return 0.5 * value * (1.0 + jnp.tanh(0.7978845608 * (value + 0.044715 * value * value * value)))

def reference(activations, up_weight, hidden_cot):
    pre = jnp.dot(activations, up_weight, preferred_element_type=jnp.float32)
    hidden = gelu_tanh(pre).astype(jnp.bfloat16)
    _, pull = jax.vjp(gelu_tanh, pre)
    slope = pull(hidden_cot.astype(jnp.float32))[0].astype(jnp.bfloat16)
    width = FF // N_COL
    slope_blocks = slope.reshape(TOKENS, N_COL, width).transpose(1, 0, 2)
    weight_blocks = up_weight.reshape(D, N_COL, width).transpose(1, 0, 2)

    def input_term(carry, pair):
        part = jnp.dot(pair[0], pair[1].T, preferred_element_type=jnp.float32).astype(jnp.bfloat16)
        part = lax.optimization_barrier(part)
        return (carry + part.astype(jnp.float32), None)
    input_total, _ = lax.scan(input_term, jnp.zeros((TOKENS, D), jnp.float32), (slope_blocks, weight_blocks))
    input_grad = input_total.astype(jnp.bfloat16)
    act_blocks = activations.reshape(N_ROW, TOK, D)
    token_slopes = slope.reshape(N_ROW, TOK, FF)

    def weight_term(carry, pair):
        part = jnp.dot(pair[0].T, pair[1], preferred_element_type=jnp.float32).astype(jnp.bfloat16)
        part = lax.optimization_barrier(part)
        return (carry + part.astype(jnp.float32), None)
    weight_total, _ = lax.scan(weight_term, jnp.zeros((D, FF), jnp.float32), (act_blocks, token_slopes))
    return (hidden, input_grad, weight_total * grad_scale)
```

```python
import jax
import jax.numpy as jnp
from jax import lax
from jax.sharding import PartitionSpec as P

grad_scale = 0.015625
cores = 2
streams = 2


def gelu_tanh(value):
    return 0.5 * value * (1.0 + jnp.tanh(0.7978845608 * (value + 0.044715 * value * value * value)))


def at(array, index, axis=0):
    return lax.dynamic_index_in_dim(array, index, axis, keepdims=False)


def wide(array):
    return array.astype(jnp.float32)


def narrow(array):
    return array.astype(jnp.bfloat16)


def on_device(activations, up_weight, hidden_cot, *, n_row, n_col):
    chips = n_col // cores
    row, col = lax.axis_index("row"), lax.axis_index("col")
    chip, core = col // cores, col % cores
    tok, width = activations.shape
    sub = tok // n_col
    depth, units = up_weight.shape
    per_chip = n_row // chips

    def across(array, flip):
        return lax.ppermute(array, "col", [(i, i ^ flip) for i in range(n_col)])

    def along(array, shift):
        return lax.ppermute(array, "row", [(i, (i + shift) % n_row) for i in range(n_row)])

    def by_core(own, other, axis):
        first = jnp.where(core == 0, own, other)
        second = jnp.where(core == 0, other, own)
        return jnp.stack([first, second], axis)

    halves = activations.reshape(chips, cores, sub, width)
    own = at(halves, core, 1)
    other = across(at(halves, 1 - core, 1), 1)
    pair = by_core(own, other, 2).reshape(chips, sub, cores * width)
    pieces = [at(pair, chip)]
    for e in range(1, chips):
        pieces.append(across(at(pair, chip ^ e), cores * e))
    fan = jnp.stack(pieces).reshape(chips, sub, per_chip, depth)

    def for_plane(plane):
        return at(at(fan, (plane // per_chip) ^ chip), plane % per_chip, 1)

    arrived = [for_plane(row)]
    for k in range(1, n_row):
        arrived.append(along(for_plane((row + k) % n_row), k))

    def gather(blocks):
        held = jnp.stack(blocks)
        laid = jnp.zeros((len(blocks), chips, sub, depth), jnp.bfloat16)
        for e in range(chips):
            piece = held if e == 0 else across(held, cores * e)
            laid = lax.dynamic_update_index_in_dim(laid, piece, chip ^ e, 1)
        return by_core(laid, across(laid, 1), 2).reshape(len(blocks), tok, depth)

    early = gather([arrived[1]])
    late = gather(arrived[2:] + arrived[:1])
    tokens = [late[-1], early[0]] + [late[i] for i in range(n_row - 2)]

    cut = units // streams
    parts = [up_weight[:, i * cut:(i + 1) * cut] for i in range(streams)]

    def term(k, i):
        return lax.dot_general(
            parts[i], tokens[k], (((0,), (1,)), ((), ())), preferred_element_type=jnp.float32
        )

    flow = [narrow(term(1, i)) for i in range(streams)]
    for k in list(range(2, n_row)) + [0]:
        flow = [along(f, 1) for f in flow]
        flow = [wide(f) + term(k, i) for i, f in enumerate(flow)]
        if k:
            flow = [narrow(f) for f in flow]

    cot = hidden_cot.T
    hidden, slopes = [], []
    for i in range(streams):
        hidden.append(narrow(gelu_tanh(flow[i])))
        _, pull = jax.vjp(gelu_tanh, flow[i])
        slopes.append(narrow(pull(wide(cot[i * cut:(i + 1) * cut]))[0]))
    hidden = jnp.concatenate(hidden).T

    ring = [slopes]
    for k in range(1, n_row):
        ring.append([along(s, 1) for s in ring[-1]])
    ring = [jnp.concatenate(s) for s in ring]

    def reduce(blocks):
        terms = [
            lax.dot_general(s, up_weight, (((0,), (1,)), ((), ())), preferred_element_type=jnp.float32)
            for s in blocks
        ]
        laid = narrow(jnp.stack(terms)).reshape(len(blocks), chips, cores, sub, depth)
        got = across(at(laid, 1 - core, 2), 1)
        mixed = narrow(wide(at(laid, core, 2)) + wide(got))
        total = wide(at(mixed, chip, 1))
        for e in range(1, chips):
            total = total + wide(across(at(mixed, chip ^ e, 1), cores * e))
        return narrow(total)

    sums = reduce(ring[:-1])
    last = reduce(ring[-1:])
    grads = [sums[k] for k in range(n_row - 1)] + [last[0]]
    placed = jnp.zeros((n_row, sub, depth), jnp.bfloat16)
    for k in range(n_row):
        block = grads[k] if k == 0 else along(grads[k], n_row - k)
        placed = lax.dynamic_update_index_in_dim(placed, block, (row + k) % n_row, 0)
    input_grad = placed.transpose(1, 0, 2).reshape(sub, n_row * depth)

    weight_grad = lax.dot_general(
        jnp.concatenate(ring, axis=1),
        jnp.concatenate(tokens, axis=0),
        (((1,), (0,)), ((), ())),
        preferred_element_type=jnp.float32,
    )
    return (hidden, input_grad, (weight_grad * grad_scale).T)


def solution(mesh):
    n_row, n_col = mesh.shape["row"], mesh.shape["col"]

    def body(activations, up_weight, hidden_cot):
        return on_device(activations, up_weight, hidden_cot, n_row=n_row, n_col=n_col)

    in_specs = (P("row", "col"), P("row", "col"), P("row", "col"))
    out_specs = (P("row", "col"), P(("row", "col"), None), P("row", "col"))
    return jax.shard_map(body, mesh=mesh, in_specs=in_specs, out_specs=out_specs, check_vma=False)
```

```python
import jax
import jax.numpy as jnp
from jax import lax
from jax.sharding import PartitionSpec as P

grad_scale = 0.015625
cores = 2
streams = 2


def gelu_tanh(value):
    return 0.5 * value * (1.0 + jnp.tanh(0.7978845608 * (value + 0.044715 * value * value * value)))


def at(array, index, axis=0):
    return lax.dynamic_index_in_dim(array, index, axis, keepdims=False)


def wide(array):
    return array.astype(jnp.float32)


def narrow(array):
    return array.astype(jnp.bfloat16)


def after(array, *others):
    return lax.optimization_barrier((array, others))[0]


def product(left, right, axes):
    return lax.dot_general(left, right, (axes, ((), ())), preferred_element_type=jnp.float32)


def on_device(activations, up_weight, hidden_cot, *, n_row, n_col):
    chips = n_col // cores
    row, col = lax.axis_index("row"), lax.axis_index("col")
    chip, core = col // cores, col % cores
    tok, width = activations.shape
    sub = tok // n_col
    depth, units = up_weight.shape
    cut = units // streams
    flipped = up_weight.T

    def across(array, flip):
        return lax.ppermute(array, "col", [(i, i ^ flip) for i in range(n_col)])

    def along(array, shift):
        return lax.ppermute(array, "row", [(i, (i + shift) % n_row) for i in range(n_row)])

    def split(array):
        return [array[i * cut:(i + 1) * cut] for i in range(streams)]

    halved = depth == cores * width
    if halved:
        shares = activations.reshape(chips, tok // chips, width)
        fan = jnp.stack(
            [at(shares, chip)] + [across(at(shares, chip ^ e), cores * e) for e in range(1, chips)]
        )

        def for_plane(plane):
            return at(fan, plane ^ chip)
    else:
        fan = lax.all_to_all(
            activations.reshape(n_col, sub, width), "col", split_axis=0, concat_axis=0, tiled=True
        )
        fan = fan.transpose(1, 0, 2).reshape(sub, n_row, depth)

        def for_plane(plane):
            return at(fan, plane, 1)

    arrived = [for_plane(row)] + [along(for_plane((row + k) % n_row), k) for k in range(1, n_row)]

    def fetch(blocks):
        held = jnp.stack(blocks)
        return [held] + [across(held, cores * e) for e in range(1, chips)]

    def lay(pieces):
        count, part, breadth = pieces[0].shape
        laid = jnp.zeros((count, chips, part, breadth), jnp.bfloat16)
        for e, piece in enumerate(pieces):
            laid = lax.dynamic_update_index_in_dim(laid, piece, chip ^ e, 1)
        return laid

    def gather(pieces):
        own, other = lay(pieces), lay([across(piece, 1) for piece in pieces])
        first, second = jnp.where(core == 0, own, other), jnp.where(core == 0, other, own)
        whole = jnp.stack([first, second], 3 if halved else 2).reshape(-1, tok, depth)
        return [whole[i] for i in range(whole.shape[0])]

    order = list(range(1, n_row)) + [0]
    early = fetch([arrived[order[0]]])
    late = fetch(after([arrived[k] for k in order[1:]], early[1]))
    tokens = gather(early) + gather(late)

    def term(j):
        return [product(part, tokens[j], ((1,), (1,))) for part in split(flipped)]

    flow = [narrow(t) for t in term(0)]
    for j in range(1, n_row):
        flow = [wide(along(f, 1)) + t for f, t in zip(flow, term(j))]
        if j < n_row - 1:
            flow = [narrow(f) for f in flow]

    hidden, slopes = [], []
    for value, cot in zip(flow, split(hidden_cot.T)):
        hidden.append(narrow(gelu_tanh(value)))
        _, pull = jax.vjp(gelu_tanh, value)
        slopes.append(narrow(pull(wide(cot))[0]))
    hidden = jnp.concatenate(hidden).T

    ring = [slopes]
    for k in range(1, n_row - 1):
        ring.append([along(s, 1) for s in ring[-1]])
    ring = [jnp.concatenate(s) for s in ring]
    ring.append(along(ring[-1], 1))

    def meet(blocks):
        terms = [narrow(product(block, flipped, ((0,), (0,)))) for block in blocks]
        laid = jnp.stack(terms).reshape(len(blocks), chips, cores, sub, depth)
        got = across(at(laid, 1 - core, 2), 1)
        return wide(at(laid, core, 2)) + wide(got)

    def fan_out(both):
        return [at(both, chip, 1)] + [narrow(at(both, chip ^ e, 1)) for e in range(1, chips)]

    def finish(parts):
        total = parts[0]
        for e in range(1, chips):
            total = total + wide(across(parts[e], cores * e))
        total = narrow(total)
        return [total[i] for i in range(total.shape[0])]

    parts = fan_out(meet(ring[:-1]))
    sums = finish(parts) + finish(fan_out(meet([after(ring[-1], parts)])))
    placed = [sums[0]] + [along(sums[k], n_row - k) for k in range(1, n_row)]
    step = 1
    while step < n_row:
        turned = [placed[(k - step) % n_row] for k in range(n_row)]
        placed = [jnp.where(row & step, t, p) for t, p in zip(turned, placed)]
        step *= 2
    input_grad = jnp.concatenate(placed, axis=1)

    weight_grad = product(
        jnp.concatenate(ring[1:] + ring[:1], axis=1), jnp.concatenate(tokens, axis=0), ((1,), (0,))
    )
    return (hidden, input_grad, (weight_grad * grad_scale).T)


def solution(mesh):
    n_row, n_col = mesh.shape["row"], mesh.shape["col"]

    def body(activations, up_weight, hidden_cot):
        return on_device(activations, up_weight, hidden_cot, n_row=n_row, n_col=n_col)

    in_specs = (P("row", "col"), P("row", "col"), P("row", "col"))
    out_specs = (P("row", "col"), P(("row", "col"), None), P("row", "col"))
    return jax.shard_map(body, mesh=mesh, in_specs=in_specs, out_specs=out_specs, check_vma=False)
```

```python
import jax
import jax.numpy as jnp
from jax import lax
from jax.sharding import PartitionSpec as P

grad_scale = 0.015625
cores = 2
streams = 2


def gelu_tanh(value):
    return 0.5 * value * (1.0 + jnp.tanh(0.7978845608 * (value + 0.044715 * value * value * value)))


def at(array, index, axis=0):
    return lax.dynamic_index_in_dim(array, index, axis, keepdims=False)


def wide(array):
    return array.astype(jnp.float32)


def narrow(array):
    return array.astype(jnp.bfloat16)


def after(array, *others):
    return lax.optimization_barrier((array, others))[0]


def product(left, right, axes):
    return lax.dot_general(left, right, (axes, ((), ())), preferred_element_type=jnp.float32)


def on_device(activations, up_weight, hidden_cot, *, n_row, n_col):
    chips = n_col // cores
    row, col = lax.axis_index("row"), lax.axis_index("col")
    chip, core = col // cores, col % cores
    tok, width = activations.shape
    sub = tok // n_col
    depth, units = up_weight.shape
    cut = units // streams
    flipped = up_weight.T

    plane_at = list(range(0, n_row, 2)) + list(range(1, n_row, 2))[::-1]
    spot_of = [plane_at.index(i) for i in range(n_row)]
    spot = jnp.where(row % 2 == 0, row // 2, n_row - 1 - row // 2)

    def plane_after(k):
        there = (spot + k) % n_row
        return jnp.where(there < (n_row + 1) // 2, 2 * there, 2 * (n_row - 1 - there) + 1)

    def across(array, flip):
        return lax.ppermute(array, "col", [(i, i ^ flip) for i in range(n_col)])

    def along(array, shift):
        pairs = [(plane_at[i], plane_at[(i + shift) % n_row]) for i in range(n_row)]
        return lax.ppermute(array, "row", pairs)

    def split(array):
        return [array[i * cut:(i + 1) * cut] for i in range(streams)]

    halved = depth == cores * width
    if halved:
        shares = activations.reshape(chips, tok // chips, width)
        fan = jnp.stack(
            [at(shares, chip)] + [across(at(shares, chip ^ e), cores * e) for e in range(1, chips)]
        )

        def for_plane(plane):
            return at(fan, plane ^ chip)
    else:
        fan = lax.all_to_all(
            activations.reshape(n_col, sub, width), "col", split_axis=0, concat_axis=0, tiled=True
        )
        fan = fan.transpose(1, 0, 2).reshape(sub, n_row, depth)

        def for_plane(plane):
            return at(fan, plane, 1)

    arrived = [for_plane(row)] + [along(for_plane(plane_after(k)), k) for k in range(1, n_row)]

    def fetch(blocks):
        held = jnp.stack(blocks)
        return [held] + [across(held, cores * e) for e in range(1, chips)]

    def lay(pieces):
        count, part, breadth = pieces[0].shape
        laid = jnp.zeros((count, chips, part, breadth), jnp.bfloat16)
        for e, piece in enumerate(pieces):
            laid = lax.dynamic_update_index_in_dim(laid, piece, chip ^ e, 1)
        return laid

    def blocks_of(whole):
        whole = whole.reshape(-1, tok, depth)
        return [whole[i] for i in range(whole.shape[0])]

    def gather_one(pieces):
        pairs = [list(range(i, i + cores)) for i in range(0, n_col, cores)]
        return blocks_of(lax.all_gather(lay(pieces), "col", axis=3 if halved else 2, axis_index_groups=pairs))

    def gather(pieces):
        others = [across(piece, 1) for piece in pieces]
        own, other = lay(pieces), lay(others)
        first, second = jnp.where(core == 0, own, other), jnp.where(core == 0, other, own)
        return blocks_of(jnp.stack([first, second], 3 if halved else 2))

    def terms_of(tokens):
        return [product(part, tokens, ((1,), (1,))) for part in split(flipped)]

    order = list(range(1, n_row)) + [0]
    early = fetch([arrived[order[0]]])
    late = fetch(after([arrived[k] for k in order[1:]], early[1]))
    tokens = gather_one(early)

    flow = [narrow(t) for t in terms_of(tokens[0])]
    for j in range(1, n_row):
        flow = [along(f, 1) for f in flow]
        if j == 1:
            tokens += gather(late)
            terms = [terms_of(t) for t in tokens[1:]]
        flow = [wide(f) + t for f, t in zip(flow, terms[j - 1])]
        if j < n_row - 1:
            flow = [narrow(f) for f in flow]

    hidden, slopes = [], []
    for value, cot in zip(flow, split(hidden_cot.T)):
        hidden.append(narrow(gelu_tanh(value)))
        _, pull = jax.vjp(gelu_tanh, value)
        slopes.append(narrow(pull(wide(cot))[0]))
    hidden = jnp.concatenate(hidden).T

    ring = [slopes]
    for k in range(1, n_row):
        if k < n_row - 1:
            ring.append([along(s, 1) for s in ring[-1]])
        else:
            ring.append(split(along(jnp.concatenate(ring[-1]), 1)))

    def meet(blocks):
        terms = [narrow(product(jnp.concatenate(b), flipped, ((0,), (0,)))) for b in blocks]
        laid = jnp.stack(terms).reshape(len(blocks), chips, cores, sub, depth)
        give = at(laid, 1 - core, 2)
        if len(blocks) == 1:
            got = across(give, 1)
        else:
            half = chips // 2
            got = jnp.concatenate([across(give[:, :half], 1), across(give[:, half:], 1)], axis=1)
        both = wide(at(laid, core, 2)) + wide(got)
        return [at(both, chip, 1)] + [narrow(at(both, chip ^ e, 1)) for e in range(1, chips)]

    def exchange(mixed):
        return mixed[:1] + [across(mixed[e], cores * e) for e in range(1, chips)]

    def finish(pieces):
        total = pieces[0]
        for piece in pieces[1:]:
            total = total + wide(piece)
        total = narrow(total)
        return [total[i] for i in range(total.shape[0])]

    pieces = [exchange(meet(ring[:-1])), exchange(meet(ring[-1:]))]
    sums = finish(pieces[0]) + finish(pieces[1])
    placed = [sums[0]] + [along(sums[k], n_row - k) for k in range(1, n_row)]
    step = 1
    while step < n_row:
        turned = [placed[(k - step) % n_row] for k in range(n_row)]
        placed = [jnp.where(spot & step, t, p) for t, p in zip(turned, placed)]
        step *= 2
    input_grad = jnp.concatenate([placed[spot_of[p]] for p in range(n_row)], axis=1)

    whole = [jnp.concatenate(s) for s in ring]
    weight_grad = product(
        jnp.concatenate(whole[1:] + whole[:1], axis=1), jnp.concatenate(tokens, axis=0), ((1,), (0,))
    )
    return (hidden, input_grad, (weight_grad * grad_scale).T)


def solution(mesh):
    n_row, n_col = mesh.shape["row"], mesh.shape["col"]

    def body(activations, up_weight, hidden_cot):
        return on_device(activations, up_weight, hidden_cot, n_row=n_row, n_col=n_col)

    in_specs = (P("row", "col"), P("row", "col"), P("row", "col"))
    out_specs = (P("row", "col"), P(("row", "col"), None), P("row", "col"))
    return jax.shard_map(body, mesh=mesh, in_specs=in_specs, out_specs=out_specs, check_vma=False)
```

```python
import jax
import jax.numpy as jnp
from jax import lax
from jax.sharding import PartitionSpec as P

grad_scale = 0.015625
cores = 2


def gelu_tanh(value):
    return 0.5 * value * (1.0 + jnp.tanh(0.7978845608 * (value + 0.044715 * value * value * value)))


def at(array, index, axis=0):
    return lax.dynamic_index_in_dim(array, index, axis, keepdims=False)


def wide(array):
    return array.astype(jnp.float32)


def narrow(array):
    return array.astype(jnp.bfloat16)


def after(array, *others):
    return lax.optimization_barrier((array, others))[0]


def product(left, right, axes):
    return lax.dot_general(left, right, (axes, ((), ())), preferred_element_type=jnp.float32)


def on_device(activations, up_weight, hidden_cot, *, n_row, n_col):
    chips = n_col // cores
    row, col = lax.axis_index("row"), lax.axis_index("col")
    chip, core = col // cores, col % cores
    tok, width = activations.shape
    sub = tok // n_col
    depth, units = up_weight.shape
    cuts = [0, (units // 2 - 32) // 16 * 16, units]
    flipped = up_weight.T

    plane_at = list(range(0, n_row, 2)) + list(range(1, n_row, 2))[::-1]
    spot_of = [plane_at.index(i) for i in range(n_row)]
    spot = jnp.where(row % 2 == 0, row // 2, n_row - 1 - row // 2)

    def plane_after(k):
        there = (spot + k) % n_row
        return jnp.where(there < (n_row + 1) // 2, 2 * there, 2 * (n_row - 1 - there) + 1)

    def across(array, flip):
        return lax.ppermute(array, "col", [(i, i ^ flip) for i in range(n_col)])

    def along(array, shift):
        pairs = [(plane_at[i], plane_at[(i + shift) % n_row]) for i in range(n_row)]
        return lax.ppermute(array, "row", pairs)

    def split(array):
        return [array[a:b] for a, b in zip(cuts, cuts[1:])]

    halved = depth == cores * width
    if halved:
        shares = activations.reshape(chips, tok // chips, width)
        fan = jnp.stack(
            [at(shares, chip)] + [across(at(shares, chip ^ e), cores * e) for e in range(1, chips)]
        )

        def for_plane(plane):
            return at(fan, plane ^ chip)
    else:
        fan = lax.all_to_all(
            activations.reshape(n_col, sub, width), "col", split_axis=0, concat_axis=0, tiled=True
        )
        fan = fan.transpose(1, 0, 2).reshape(sub, n_row, depth)

        def for_plane(plane):
            return at(fan, plane, 1)

    arrived = [for_plane(row)] + [along(for_plane(plane_after(k)), k) for k in range(1, n_row)]

    def fetch(blocks):
        held = jnp.stack(blocks)
        return [held] + [across(held, cores * e) for e in range(1, chips)]

    def lay(pieces):
        count, part, breadth = pieces[0].shape
        laid = jnp.zeros((count, chips, part, breadth), jnp.bfloat16)
        for e, piece in enumerate(pieces):
            laid = lax.dynamic_update_index_in_dim(laid, piece, chip ^ e, 1)
        return laid

    def blocks_of(whole):
        whole = whole.reshape(-1, tok, depth)
        return [whole[i] for i in range(whole.shape[0])]

    def gather_one(pieces):
        pairs = [list(range(i, i + cores)) for i in range(0, n_col, cores)]
        return blocks_of(lax.all_gather(lay(pieces), "col", axis=3 if halved else 2, axis_index_groups=pairs))

    def gather(pieces):
        others = [across(piece, 1) for piece in pieces]
        own, other = lay(pieces), lay(others)
        first, second = jnp.where(core == 0, own, other), jnp.where(core == 0, other, own)
        return blocks_of(jnp.stack([first, second], 3 if halved else 2))

    def terms_of(tokens):
        return [product(part, tokens, ((1,), (1,))) for part in split(flipped)]

    order = list(range(1, n_row)) + [0]
    early = fetch([arrived[order[0]]])
    late = fetch(after([arrived[k] for k in order[1:]], early[1]))
    tokens = gather_one(early)

    flow = [narrow(t) for t in terms_of(tokens[0])]
    for j in range(1, n_row):
        flow = [along(f, 1) for f in flow]
        if j == 1:
            tokens += gather(late)
            terms = [terms_of(t) for t in tokens[1:]]
        flow = [wide(f) + t for f, t in zip(flow, terms[j - 1])]
        if j < n_row - 1:
            flow = [narrow(f) for f in flow]

    hidden, slopes = [], []
    for value, cot in zip(flow, split(hidden_cot.T)):
        hidden.append(narrow(gelu_tanh(value)))
        _, pull = jax.vjp(gelu_tanh, value)
        slopes.append(narrow(pull(wide(cot))[0]))
    hidden = jnp.concatenate(hidden).T

    ring = [slopes]
    for k in range(1, n_row):
        if k < n_row - 1:
            ring.append([along(s, n_row - 1) for s in ring[-1]])
        else:
            ring.append(split(along(jnp.concatenate(ring[-1]), n_row - 1)))

    def meet(blocks):
        terms = [narrow(product(jnp.concatenate(b), flipped, ((0,), (0,)))) for b in blocks]
        laid = jnp.stack(terms).reshape(len(blocks), chips, cores, sub, depth)
        give = at(laid, 1 - core, 2)
        if len(blocks) == 1:
            got = across(give, 1)
        else:
            half = chips // 2
            got = jnp.concatenate([across(give[:, :half], 1), across(give[:, half:], 1)], axis=1)
        both = wide(at(laid, core, 2)) + wide(got)
        return [at(both, chip, 1)] + [narrow(at(both, chip ^ e, 1)) for e in range(1, chips)]

    def exchange(mixed):
        return mixed[:1] + [across(mixed[e], cores * e) for e in range(1, chips)]

    def finish(pieces):
        total = pieces[0]
        for piece in pieces[1:]:
            total = total + wide(piece)
        total = narrow(total)
        return [total[i] for i in range(total.shape[0])]

    pieces = [exchange(meet(ring[:-1])), exchange(meet(ring[-1:]))]
    sums = finish(pieces[0]) + finish(pieces[1])
    placed = [None] * n_row
    for k in range(n_row):
        placed[(n_row - k) % n_row] = along(sums[k], k) if k else sums[k]
    step = 1
    while step < n_row:
        turned = [placed[(k - step) % n_row] for k in range(n_row)]
        placed = [jnp.where(spot & step, t, p) for t, p in zip(turned, placed)]
        step *= 2
    input_grad = jnp.concatenate([placed[spot_of[p]] for p in range(n_row)], axis=1)

    whole = [jnp.concatenate(s) for s in ring]
    weight_grad = product(
        jnp.concatenate(whole[:0:-1] + whole[:1], axis=1), jnp.concatenate(tokens, axis=0), ((1,), (0,))
    )
    return (hidden, input_grad, (weight_grad * grad_scale).T)


def solution(mesh):
    n_row, n_col = mesh.shape["row"], mesh.shape["col"]

    def body(activations, up_weight, hidden_cot):
        return on_device(activations, up_weight, hidden_cot, n_row=n_row, n_col=n_col)

    in_specs = (P("row", "col"), P("row", "col"), P("row", "col"))
    out_specs = (P("row", "col"), P(("row", "col"), None), P("row", "col"))
    return jax.shard_map(body, mesh=mesh, in_specs=in_specs, out_specs=out_specs, check_vma=False)
```

```python
import jax
import jax.numpy as jnp
from jax import lax
from jax.sharding import PartitionSpec as P

grad_scale = 0.015625
cores = 2


def gelu_tanh(value):
    return 0.5 * value * (1.0 + jnp.tanh(0.7978845608 * (value + 0.044715 * value * value * value)))


def at(array, index, axis=0):
    return lax.dynamic_index_in_dim(array, index, axis, keepdims=False)


def wide(array):
    return array.astype(jnp.float32)


def narrow(array):
    return array.astype(jnp.bfloat16)


def after(array, *others):
    return lax.optimization_barrier((array, others))[0]


def product(left, right, axes):
    return lax.dot_general(left, right, (axes, ((), ())), preferred_element_type=jnp.float32)


def on_device(activations, up_weight, hidden_cot, *, n_row, n_col):
    chips = n_col // cores
    row, col = lax.axis_index("row"), lax.axis_index("col")
    chip, core = col // cores, col % cores
    tok, width = activations.shape
    sub = tok // n_col
    depth, units = up_weight.shape
    cuts = [0, (units // 2 - 32) // 16 * 16, units]
    flipped = up_weight.T

    plane_at = list(range(0, n_row, 2)) + list(range(1, n_row, 2))[::-1]
    spot_of = [plane_at.index(i) for i in range(n_row)]
    spot = jnp.where(row % 2 == 0, row // 2, n_row - 1 - row // 2)

    def plane_after(k):
        there = (spot + k) % n_row
        return jnp.where(there < (n_row + 1) // 2, 2 * there, 2 * (n_row - 1 - there) + 1)

    def across(array, flip):
        return lax.ppermute(array, "col", [(i, i ^ flip) for i in range(n_col)])

    def along(array, shift):
        pairs = [(plane_at[i], plane_at[(i + shift) % n_row]) for i in range(n_row)]
        return lax.ppermute(array, "row", pairs)

    def split(array):
        return [array[a:b] for a, b in zip(cuts, cuts[1:])]

    halved = depth == cores * width
    if halved:
        shares = activations.reshape(chips, tok // chips, width)
        fan = jnp.stack(
            [at(shares, chip)] + [across(at(shares, chip ^ e), cores * e) for e in range(1, chips)]
        )

        def for_plane(plane):
            return at(fan, plane ^ chip)
    else:
        fan = lax.all_to_all(
            activations.reshape(n_col, sub, width), "col", split_axis=0, concat_axis=0, tiled=True
        )
        fan = fan.transpose(1, 0, 2).reshape(sub, n_row, depth)

        def for_plane(plane):
            return at(fan, plane, 1)

    arrived = [for_plane(row)] + [along(for_plane(plane_after(k)), k) for k in range(1, n_row)]

    def fetch(blocks):
        held = jnp.stack(blocks)
        return [held] + [across(held, cores * e) for e in range(1, chips)]

    def lay(pieces):
        count, part, breadth = pieces[0].shape
        laid = jnp.zeros((count, chips, part, breadth), jnp.bfloat16)
        for e, piece in enumerate(pieces):
            laid = lax.dynamic_update_index_in_dim(laid, piece, chip ^ e, 1)
        return laid

    def blocks_of(whole):
        whole = whole.reshape(-1, tok, depth)
        return [whole[i] for i in range(whole.shape[0])]

    def gather_one(pieces):
        pairs = [list(range(i, i + cores)) for i in range(0, n_col, cores)]
        return blocks_of(lax.all_gather(lay(pieces), "col", axis=3 if halved else 2, axis_index_groups=pairs))

    def gather(pieces):
        others = [across(piece, 1) for piece in pieces]
        own, other = lay(pieces), lay(others)
        first, second = jnp.where(core == 0, own, other), jnp.where(core == 0, other, own)
        return blocks_of(jnp.stack([first, second], 3 if halved else 2))

    def terms_of(tokens):
        return [product(part, tokens, ((1,), (1,))) for part in split(flipped)]

    order = list(range(1, n_row)) + [0]
    early = fetch([arrived[order[0]]])
    late = fetch(after([arrived[k] for k in order[1:]], early[1]))
    tokens = gather_one(early)

    flow = [narrow(t) for t in terms_of(tokens[0])]
    for j in range(1, n_row):
        flow = [along(f, 1) for f in flow]
        if j == 1:
            tokens += gather(late)
            terms = [terms_of(t) for t in tokens[1:]]
        flow = [wide(f) + t for f, t in zip(flow, terms[j - 1])]
        if j < n_row - 1:
            flow = [narrow(f) for f in flow]

    hidden, slopes = [], []
    for value, cot in zip(flow, split(hidden_cot.T)):
        hidden.append(narrow(gelu_tanh(value)))
        _, pull = jax.vjp(gelu_tanh, value)
        slopes.append(narrow(pull(wide(cot))[0]))
    hidden = jnp.concatenate(hidden).T

    ring = [slopes]
    for k in range(1, n_row):
        if k < n_row - 1:
            ring.append([along(s, n_row - 1) for s in ring[-1]])
        else:
            ring.append(split(along(jnp.concatenate(ring[-1]), n_row - 1)))

    def meet(blocks):
        terms = [narrow(product(jnp.concatenate(b), flipped, ((0,), (0,)))) for b in blocks]
        laid = jnp.stack(terms).reshape(len(blocks), chips, cores, sub, depth)
        give = at(laid, 1 - core, 2)
        if len(blocks) == 1:
            got = across(give, 1)
        else:
            half = chips // 2
            got = jnp.concatenate([across(give[:, :half], 1), across(give[:, half:], 1)], axis=1)
        both = wide(at(laid, core, 2)) + wide(got)
        return [at(both, chip, 1)] + [narrow(at(both, chip ^ e, 1)) for e in range(1, chips)]

    def exchange(mixed):
        return mixed[:1] + [across(mixed[e], cores * e) for e in range(1, chips)]

    def finish(pieces):
        total = pieces[0]
        for piece in pieces[1:]:
            total = total + wide(piece)
        total = narrow(total)
        return [total[i] for i in range(total.shape[0])]

    pieces = [exchange(meet(blocks)) for blocks in (ring[:-2], ring[-2:-1], ring[-1:])]

    whole = [jnp.concatenate(s) for s in ring]
    weight_grad = grad_scale * product(
        jnp.concatenate(whole[:0:-1] + whole[:1], axis=1), jnp.concatenate(tokens, axis=0), ((1,), (0,))
    )
    pieces[-1][1:] = after(pieces[-1][1:], weight_grad)

    sums = [total for batch in pieces for total in finish(batch)]
    placed = [None] * n_row
    for k in range(n_row):
        placed[(n_row - k) % n_row] = along(sums[k], k) if k else sums[k]
    step = 1
    while step < n_row:
        turned = [placed[(k - step) % n_row] for k in range(n_row)]
        placed = [jnp.where(spot & step, t, p) for t, p in zip(turned, placed)]
        step *= 2
    input_grad = jnp.concatenate([placed[spot_of[p]] for p in range(n_row)], axis=1)

    return (hidden, input_grad, weight_grad.T)


def solution(mesh):
    n_row, n_col = mesh.shape["row"], mesh.shape["col"]

    def body(activations, up_weight, hidden_cot):
        return on_device(activations, up_weight, hidden_cot, n_row=n_row, n_col=n_col)

    in_specs = (P("row", "col"), P("row", "col"), P("row", "col"))
    out_specs = (P("row", "col"), P(("row", "col"), None), P("row", "col"))
    return jax.shard_map(body, mesh=mesh, in_specs=in_specs, out_specs=out_specs, check_vma=False)
```

```python
import jax
import jax.numpy as jnp
from jax import lax
from jax.sharding import PartitionSpec as P

grad_scale = 0.015625
cores = 2


def gelu_tanh(value):
    return 0.5 * value * (1.0 + jnp.tanh(0.7978845608 * (value + 0.044715 * value * value * value)))


def at(array, index, axis=0):
    return lax.dynamic_index_in_dim(array, index, axis, keepdims=False)


def wide(array):
    return array.astype(jnp.float32)


def narrow(array):
    return array.astype(jnp.bfloat16)


def after(array, *others):
    return lax.optimization_barrier((array, others))[0]


def product(left, right, axes):
    return lax.dot_general(left, right, (axes, ((), ())), preferred_element_type=jnp.float32)


def on_device(activations, up_weight, hidden_cot, *, n_row, n_col):
    chips = n_col // cores
    row, col = lax.axis_index("row"), lax.axis_index("col")
    chip, core = col // cores, col % cores
    tok, width = activations.shape
    sub = tok // n_col
    depth, units = up_weight.shape
    cuts = [0, (units // 2 - 16) // 16 * 16, units]
    flipped = up_weight.T

    plane_at = list(range(0, n_row, 2)) + list(range(1, n_row, 2))[::-1]
    spot_of = [plane_at.index(i) for i in range(n_row)]
    spot = jnp.where(row % 2 == 0, row // 2, n_row - 1 - row // 2)

    def plane_after(k):
        there = (spot + k) % n_row
        return jnp.where(there < (n_row + 1) // 2, 2 * there, 2 * (n_row - 1 - there) + 1)

    def across(array, flip):
        return lax.ppermute(array, "col", [(i, i ^ flip) for i in range(n_col)])

    def along(array, shift):
        pairs = [(plane_at[i], plane_at[(i + shift) % n_row]) for i in range(n_row)]
        return lax.ppermute(array, "row", pairs)

    def split(array):
        return [array[a:b] for a, b in zip(cuts, cuts[1:])]

    halved = depth == cores * width
    if halved:
        shares = activations.reshape(chips, tok // chips, width)
        fan = jnp.stack(
            [at(shares, chip)] + [across(at(shares, chip ^ e), cores * e) for e in range(1, chips)]
        )

        def for_plane(plane):
            return at(fan, plane ^ chip)
    else:
        fan = lax.all_to_all(
            activations.reshape(n_col, sub, width), "col", split_axis=0, concat_axis=0, tiled=True
        )
        fan = fan.transpose(1, 0, 2).reshape(sub, n_row, depth)

        def for_plane(plane):
            return at(fan, plane, 1)

    arrived = [for_plane(row)] + [along(for_plane(plane_after(k)), k) for k in range(1, n_row)]

    def fetch(blocks):
        held = jnp.stack(blocks)
        return [held] + [across(held, cores * e) for e in range(chips - 1, 0, -1)][::-1]

    def lay(pieces):
        count, part, breadth = pieces[0].shape
        laid = jnp.zeros((count, chips, part, breadth), jnp.bfloat16)
        for e, piece in enumerate(pieces):
            laid = lax.dynamic_update_index_in_dim(laid, piece, chip ^ e, 1)
        return laid

    def blocks_of(whole):
        whole = whole.reshape(-1, tok, depth)
        return [whole[i] for i in range(whole.shape[0])]

    def gather_one(pieces):
        pairs = [list(range(i, i + cores)) for i in range(0, n_col, cores)]
        whole = lax.all_gather(lay(pieces), "col", axis=3 if halved else 2, axis_index_groups=pairs)
        tokens = blocks_of(whole)
        if not halved:
            return tokens, terms_of(tokens[0])
        sides = [whole[0, :, :, k].reshape(tok, width) for k in range(cores)]
        return tokens, [
            sum(product(part[:, k * width:(k + 1) * width], sides[k], ((1,), (1,))) for k in range(cores))
            for part in split(flipped)
        ]

    def gather(pieces):
        others = [across(piece, 1) for piece in pieces]
        own, other = lay(pieces), lay(others)
        first, second = jnp.where(core == 0, own, other), jnp.where(core == 0, other, own)
        return blocks_of(jnp.stack([first, second], 3 if halved else 2))

    def terms_of(tokens):
        return [product(part, tokens, ((1,), (1,))) for part in split(flipped)]

    order = list(range(1, n_row)) + [0]
    early = fetch([arrived[order[0]]])
    late = fetch(after([arrived[k] for k in order[1:]], early[1]))
    tokens, first_terms = gather_one(early)

    flow = [narrow(t) for t in first_terms]
    for j in range(1, n_row):
        flow = [along(f, 1) for f in flow]
        if j == 1:
            tokens += gather(late)
            terms = [terms_of(t) for t in tokens[1:]]
        flow = [wide(f) + t for f, t in zip(flow, terms[j - 1])]
        if j < n_row - 1:
            flow = [narrow(f) for f in flow]

    hidden, slopes = [], []
    for value, cot in zip(flow, split(hidden_cot.T)):
        hidden.append(narrow(gelu_tanh(value)))
        _, pull = jax.vjp(gelu_tanh, value)
        slopes.append(narrow(pull(wide(cot))[0]))
    hidden = jnp.concatenate(hidden).T

    ring = [slopes]
    for k in range(1, n_row):
        if k < n_row - 1:
            ring.append([along(s, n_row - 1) for s in ring[-1]])
        else:
            ring.append(split(along(jnp.concatenate(ring[-1]), n_row - 1)))

    def meet(blocks):
        terms = [narrow(product(jnp.concatenate(b), flipped, ((0,), (0,)))) for b in blocks]
        laid = jnp.stack(terms).reshape(len(blocks), chips, cores, sub, depth)
        give = at(laid, 1 - core, 2)
        if len(blocks) == 1:
            got = across(give, 1)
        else:
            half = chips // 2
            got = jnp.concatenate([across(give[:, :half], 1), across(give[:, half:], 1)], axis=1)
        both = wide(at(laid, core, 2)) + wide(got)
        return [at(both, chip, 1)] + [narrow(at(both, chip ^ e, 1)) for e in range(1, chips)]

    def exchange(mixed):
        return mixed[:1] + [across(mixed[e], cores * e) for e in range(1, chips)]

    def finish(pieces):
        total = pieces[0]
        for piece in pieces[1:]:
            total = total + wide(piece)
        total = narrow(total)
        return [total[i] for i in range(total.shape[0])]

    pieces = [exchange(meet(blocks)) for blocks in (ring[:-2], ring[-2:-1], ring[-1:])]

    whole = [jnp.concatenate(s) for s in ring]
    weight_grad = grad_scale * product(
        jnp.concatenate(whole[:0:-1] + whole[:1], axis=1), jnp.concatenate(tokens, axis=0), ((1,), (0,))
    )
    pieces[-1][1:] = after(pieces[-1][1:], weight_grad)

    sums = [total for batch in pieces for total in finish(batch)]
    placed = [None] * n_row
    for k in range(n_row):
        placed[(n_row - k) % n_row] = along(sums[k], k) if k else sums[k]
    step = 1
    while step < n_row:
        turned = [placed[(k - step) % n_row] for k in range(n_row)]
        placed = [jnp.where(spot & step, t, p) for t, p in zip(turned, placed)]
        step *= 2
    input_grad = jnp.concatenate([placed[spot_of[p]] for p in range(n_row)], axis=1)

    return (hidden, input_grad, weight_grad.T)


def solution(mesh):
    n_row, n_col = mesh.shape["row"], mesh.shape["col"]

    def body(activations, up_weight, hidden_cot):
        return on_device(activations, up_weight, hidden_cot, n_row=n_row, n_col=n_col)

    in_specs = (P("row", "col"), P("row", "col"), P("row", "col"))
    out_specs = (P("row", "col"), P(("row", "col"), None), P("row", "col"))
    return jax.shard_map(body, mesh=mesh, in_specs=in_specs, out_specs=out_specs, check_vma=False)
```
